256 devices in a mesh: dp: 32 (over z, x), vocab: 8 (over y, core).
Axes of the slice: x: 4, y: 4, z: 8, core: 2. Of those that a mesh axis runs over, the one named last changes fastest.
Arguments:
- hidden_states: bfloat16 [4096, 3584], P('dp'), may hold values from -40 to 40
- head_weight: bfloat16 [3584, 98304], P(None, ('dp', 'vocab')), as said below
- target_ids: int32 [4096], replicated, may hold values from 0 to 98303
- seq_lengths: int32 [256], P('dp'), may hold values from 1 to 16
- domain_labels: int32 [256], P('dp'), may hold values from 0 to 21
- domain_weights: float32 [22], replicated, may hold values from 0.5 to 4
Outputs:
- token_loss: float32 [4096], P('dp')
- new_weights: float32 [22], replicated
The draws below stay inside these ranges and needn't reach their ends.
Inputs may be any that keep to these rules, and one draw needn't show every extreme that they name: `head_weight`: every entry lies within 6 / sqrt(3584) of zero.
All inputs are finite; a program needn't handle non-finite values.
Results may differ from the reference program's by a relative error of at most 0.0003.
Values may be sent and summed in bfloat16 or wider, within the bound.
No kernel may reach another device: no remote copies, remote signals or barrier semaphores. Data moves between devices by JAX's collectives and lax.ppermute only.
A program may use at most 128 MiB of HBM per device.

```python
import math
import jax
import jax.numpy as jnp
import numpy as np
from jax import lax

D = 3584
VOCAB = 98304
SEQ_LEN = 16
DOMAINS = 22
SEQS = 256
TOKENS = 4096
N_DP = 32


def weight_table(key):
    base = jax.random.normal(jax.random.fold_in(key, 11), (D, VOCAB), jnp.float32)
    return jnp.clip(base, -6.0, 6.0) / math.sqrt(D)


def draw_head_weight(key, part):
    return weight_table(key).astype(jnp.bfloat16)


def draw_hidden_states(key, part):
    base = jax.random.normal(jax.random.fold_in(key, 31), (TOKENS, D), jnp.float32)
    return jnp.clip(3.0 * base, -18.0, 18.0).astype(jnp.bfloat16)


def plant(entries, own_key, least, high):
    dims = entries.shape
    spot = [jax.random.randint(jax.random.fold_in(own_key, axis), (), 0, dims[axis]) for axis in range(len(dims))]
    entries = entries.at[tuple(spot)].set(least)
    longest = dims.index(max(dims))
    spot[longest] = (spot[longest] + 1) % dims[longest]
    return entries.at[tuple(spot)].set(high)


def cumulative_ranks(number_of, lean):
    portions = [(1 << 20) // math.isqrt(standing ** lean) + 1 for standing in range(1, number_of + 1)]
    deviation = 1 + sum(portions) // (1 << 30)
    return np.cumsum(np.array([max(1, weight // deviation) for weight in portions]))


def skewed_ids(stream_key, extent, count, lean):
    grid = cumulative_ranks(count, lean)
    lot = jax.random.randint(jax.random.fold_in(stream_key, 1), extent, 0, int(grid[count - 1]))
    grade = jnp.searchsorted(jnp.asarray(grid, jnp.int32), lot, side="right")
    return jax.random.permutation(jax.random.fold_in(stream_key, 2), count)[grade].astype(jnp.int32)


def setup_inputs(seed: int = 0) -> dict:
    seeds = jax.random.split(jax.random.key(seed), 7)
    hidden_states = draw_hidden_states(jax.random.fold_in(seeds[6], 71), 0)
    head_weight = draw_head_weight(jax.random.fold_in(seeds[6], 71), 0)
    target_ids = plant(jax.random.randint(seeds[2], (TOKENS,), 0, VOCAB), jax.random.fold_in(seeds[2], 1), 0, VOCAB - 1).astype(jnp.int32)
    seq_lengths = plant(jax.random.randint(seeds[3], (SEQS,), 1, SEQ_LEN + 1), jax.random.fold_in(seeds[3], 1), 1, SEQ_LEN).astype(jnp.int32)
    domain_labels = plant(skewed_ids(seeds[4], (SEQS,), DOMAINS, 2), jax.random.fold_in(seeds[4], 3), 0, DOMAINS - 1).astype(jnp.int32)
    domain_weights = jnp.clip(jnp.exp(jax.random.uniform(seeds[5], (DOMAINS,), jnp.float32, math.log(0.5), math.log(4.0))), 0.5, 4.0)
    return dict(hidden_states=hidden_states, head_weight=head_weight, target_ids=target_ids, seq_lengths=seq_lengths, domain_labels=domain_labels, domain_weights=domain_weights)


explore_share = 0.01
step_rate = 0.002


def reference(hidden_states, head_weight, target_ids, seq_lengths, domain_labels, domain_weights):
    def block_loss(block):
        block_rows, targets = block
        logits = jnp.dot(block_rows, head_weight, preferred_element_type=jnp.float32)
        row_peak = jnp.max(logits, axis=1)
        mass_sum = jnp.sum(jnp.exp(logits - row_peak[:, None]), axis=1)
        picked = jnp.take_along_axis(logits, targets[:, None], axis=1)[:, 0]
        return jnp.log(mass_sum) + row_peak - picked

    blocks = (hidden_states.reshape(N_DP, -1, D), target_ids.reshape(N_DP, -1))
    raw_loss = lax.map(block_loss, blocks).reshape(-1)
    positions = jnp.arange(TOKENS) % SEQ_LEN
    valid = positions < jnp.repeat(seq_lengths, SEQ_LEN)
    token_loss = jnp.where(valid, raw_loss, 0.0)
    seq_loss = jnp.sum(token_loss.reshape(-1, SEQ_LEN), axis=1)
    seq_tokens = seq_lengths.astype(jnp.float32)
    domain_hot = (domain_labels[:, None] == jnp.arange(DOMAINS)[None, :]).astype(jnp.float32)
    domain_loss = jnp.sum(domain_hot * seq_loss[:, None], axis=0)
    domain_count = jnp.sum(domain_hot * seq_tokens[:, None], axis=0)
    probability = (1.0 - DOMAINS * explore_share) * domain_weights / jnp.sum(domain_weights) + explore_share
    reward = domain_loss / jnp.maximum(domain_count, 1.0) / probability
    raised = domain_weights * jnp.exp(step_rate * reward)
    new_weights = DOMAINS * raised / jnp.sum(raised)
    return token_loss, new_weights
```

```python
import functools
import jax
import jax.numpy as jnp
from jax import lax
from jax.experimental import pallas as pl
from jax.experimental.pallas import tpu as pltpu
from jax.sharding import Mesh
from jax.sharding import PartitionSpec as P

SEQ_LEN = 16
DOMAINS = 22
explore_share = 0.01
step_rate = 0.002

ALL = ("z", "x", "yh", "yl", "c")
DP = ("z", "x")
VOCAB_AXES = ("yh", "yl", "c")
SUB = 16


def shift(a, axis, by):
    n = lax.axis_size(axis)
    return lax.ppermute(a, axis, [(i, (i + by) % n) for i in range(n)])


def lane_parts(a):
    return [a[:, i : i + 128] for i in range(0, a.shape[1], 128)]


def stats_kernel(nb, np_, rows, starts, targets, *refs):
    blocks = refs[:nb]
    cols = refs[nb : nb + 2 * np_]
    out = refs[nb + 2 * np_]
    h_vm, w_vm, t_vm, m_vm, s_vm, p_vm, h_sem, w_sem = refs[nb + 2 * np_ + 1 :]
    height = blocks[0].shape[0]
    width = cols[0].shape[1]
    h_copies = [
        pltpu.make_async_copy(b, h_vm.at[pl.ds(i * height, height)], h_sem.at[i])
        for i, b in enumerate(blocks)
    ]
    w_copies = [
        pltpu.make_async_copy(w, w_vm.at[k // 2, :, pl.ds((k % 2) * width, width)], w_sem.at[k])
        for k, w in enumerate(cols)
    ]
    for copy in h_copies + w_copies:
        copy.start()
    total = nb * height
    spread = jnp.broadcast_to(targets[...].astype(jnp.float32), (128, total))
    t_vm[...] = spread.T.astype(jnp.int32)
    for copy in h_copies:
        copy.wait()
    for j in range(np_):
        w_copies[2 * j].wait()
        w_copies[2 * j + 1].wait()
        first, second = starts[2 * j], starts[2 * j + 1]

        @pl.loop(0, total // rows)
        def _(r):
            here = pl.ds(pl.multiple_of(r * rows, rows), rows)
            logits = jnp.dot(h_vm[here], w_vm[j], preferred_element_type=jnp.float32)
            parts = lane_parts(logits)
            peak = functools.reduce(jnp.maximum, parts)
            if j:
                before = m_vm[here]
                peak = jnp.maximum(peak, before)
                mass = s_vm[here] * jnp.exp(before - peak)
                pick = p_vm[here]
            else:
                mass = jnp.zeros_like(peak)
                pick = jnp.zeros_like(peak)
            away = t_vm[here] - lax.broadcasted_iota(jnp.int32, peak.shape, 1)
            for i, part in enumerate(parts):
                at = i * 128
                column = first + at if at < width else second + (at - width)
                mass = mass + jnp.exp(part - peak)
                pick = pick + jnp.where(away == column, part, 0.0)
            m_vm[here] = peak
            s_vm[here] = mass
            p_vm[here] = pick

    lane_peak = m_vm[...].T
    peak = jnp.max(lane_peak, axis=0, keepdims=True)
    mass = jnp.sum(s_vm[...].T * jnp.exp(lane_peak - peak), axis=0, keepdims=True)
    pick = jnp.sum(p_vm[...].T, axis=0, keepdims=True)
    out[0:1, :] = peak + jnp.log(mass)
    out[1:2, :] = pick


def tile_stats(blocks, targets, cols, starts):
    nb, np_ = len(blocks), len(cols) // 2
    height, depth = blocks[0].shape
    width = cols[0].shape[1]
    total = nb * height
    rows = 128
    any_spec = pl.BlockSpec(memory_space=pl.ANY)
    return pl.pallas_call(
        functools.partial(stats_kernel, nb, np_, rows),
        out_shape=jax.ShapeDtypeStruct((2, total), jnp.float32),
        in_specs=[
            pl.BlockSpec(memory_space=pltpu.SMEM),
            pl.BlockSpec(memory_space=pltpu.VMEM),
        ]
        + [any_spec] * (nb + 2 * np_),
        out_specs=pl.BlockSpec(memory_space=pltpu.VMEM),
        scratch_shapes=[
            pltpu.VMEM((total, depth), jnp.bfloat16),
            pltpu.VMEM((np_, depth, 2 * width), jnp.bfloat16),
            pltpu.VMEM((total, 128), jnp.int32),
            pltpu.VMEM((total, 128), jnp.float32),
            pltpu.VMEM((total, 128), jnp.float32),
            pltpu.VMEM((total, 128), jnp.float32),
            pltpu.SemaphoreType.DMA((nb,)),
            pltpu.SemaphoreType.DMA((2 * np_,)),
        ],
        compiler_params=pltpu.CompilerParams(vmem_limit_bytes=40 * 2**20),
        cost_estimate=pl.CostEstimate(
            flops=2 * total * depth * 2 * np_ * width,
            bytes_accessed=2 * depth * (total + 2 * np_ * width),
            transcendentals=total * 2 * np_ * width,
        ),
    )(starts, targets.reshape(1, total), *blocks, *cols)


def rolled(a, axis, by):
    n = a.shape[axis]
    twice = jnp.concatenate([a, a], axis=axis)
    return lax.dynamic_slice_in_dim(twice, by, n, axis)


def merged(lse, axis):
    top = jnp.max(lse, axis=axis, keepdims=True)
    return jnp.squeeze(top, axis) + jnp.log(jnp.sum(jnp.exp(lse - top), axis=axis))


def body(hidden_states, head_weight, target_ids, seq_lengths, domain_labels, domain_weights):
    z, x = lax.axis_index("z"), lax.axis_index("x")
    yh, yl, c = (lax.axis_index(a) for a in VOCAB_AXES)
    nz, nx = lax.axis_size("z"), lax.axis_size("x")
    dp_count = nz * nx
    dp_index = z * nx + x
    y = yh * 2 + yl
    quarter = yl * 2 + c
    share = hidden_states.shape[0] // 4
    width = head_weight.shape[1]

    own = lax.dynamic_slice_in_dim(hidden_states, quarter * share, share, 0)
    a, b = own[:SUB], own[SUB:]

    moves = [
        (k * 2 + core, ((k + (1 if core == 0 else -1)) % 4) * 2 + core)
        for k in range(4)
        for core in range(2)
    ]
    col_in = lax.ppermute(head_weight, VOCAB_AXES, moves)
    col_mate = shift(head_weight, "c", 1)

    a_m, a_p, a_o = shift(a, "x", 1), shift(a, "x", -1), shift(a, "x", 2)
    a1 = jnp.concatenate([a, a_m, a_p, a_o], axis=0)
    zm, zp = [a1], [a1]
    bm, bp = [b], [b]
    for _ in range(3):
        bm.append(shift(bm[-1], "z", 1))
        bp.append(shift(bp[-1], "z", -1))
    b4 = shift(bp[3], "z", -1)
    half_1 = jnp.concatenate([b, bm[1], bp[1], bm[2]], axis=0)
    half_2 = jnp.concatenate([bp[2], bm[3], bp[3], b4], axis=0)
    for _ in range(3):
        zm.append(shift(zm[-1], "z", 1))
        zp.append(shift(zp[-1], "z", -1))
    z4 = jnp.concatenate(
        [shift(zm[3][: 2 * SUB], "z", 1), shift(zp[3][2 * SUB :], "z", -1)], axis=0
    )
    h1m, h1p = shift(half_1, "x", 1), shift(half_1, "x", -1)
    h2m, h2p = shift(half_2, "x", 1), shift(half_2, "x", -1)
    h1o, h2o = shift(h1m, "x", 1), shift(h2p, "x", -1)
    col_in_mate = shift(col_in, "c", 1)

    dx_order = (0, nx - 1, 1, 2)
    z_blocks = [(a1, 0)]
    for k in range(1, 4):
        z_blocks += [(zm[k], nz - k), (zp[k], k)]
    z_blocks.append((z4, 4))
    half_dz = ((0, nz - 1, 1, nz - 2), (2, nz - 3, 3, 4))
    x_blocks = [
        (block, half_dz[h], dx)
        for h, four in enumerate(((half_1, h1m, h1p, h1o), (half_2, h2m, h2p, h2o)))
        for block, dx in zip(four, dx_order)
    ]
    order = []
    for block, dz in z_blocks:
        order.append((block, [(dz, dx, 0) for dx in dx_order]))
    for block, dzs, dx in x_blocks:
        order.append((block, [(dz, dx, 1) for dz in dzs]))
    groups = [(0, 1, 2, 8, 9, 10, 12, 3), (4, 13, 14, 11, 5, 6, 15, 7)]

    targets = target_ids.reshape(nz, nx, 4, 2, SUB)
    targets = lax.dynamic_index_in_dim(targets, quarter, 2, keepdims=False)
    targets = rolled(rolled(targets, 0, z), 1, x)

    def start_of(y_at, core):
        return (dp_index * 8 + (y_at % 4) * 2 + core) * width

    def start_in(core):
        return jnp.where(core == 0, start_of(y + 3, 0), start_of(y + 1, 1))

    starts = jnp.stack([start_of(y, c), start_of(y, 1 - c), start_in(c), start_in(1 - c)])
    cols = [head_weight, col_mate, col_in, col_in_mate]

    found = {}
    for group in groups:
        subs = [s for g in group for s in order[g][1]]
        wanted = jnp.concatenate([targets[s] for s in subs])
        stats = tile_stats([order[g][0] for g in group], wanted, cols, starts.astype(jnp.int32))
        for i, s in enumerate(subs):
            found[s] = stats[:, i * SUB : (i + 1) * SUB]
    every = jnp.stack(
        [
            jnp.concatenate([found[dz, dx, 0], found[dz, dx, 1]], axis=1)
            for dz in range(nz)
            for dx in range(nx)
        ]
    )
    every = every.reshape(nz, nx, -1)
    every = rolled(rolled(every, 0, (nz - z) % nz), 1, (nx - x) % nx).reshape(dp_count, -1)
    mine = lax.all_to_all(every, DP, 0, 0, tiled=True)
    lse = merged(mine[:, :share], 0)
    pick = jnp.sum(mine[:, share:], axis=0)
    note = jnp.concatenate(
        [lse, pick, seq_lengths.astype(jnp.float32), domain_labels.astype(jnp.float32)]
    )
    note = jnp.concatenate([note, jnp.zeros((128 - note.shape[0],), jnp.float32)])
    sent = jnp.broadcast_to(note[None], (lax.axis_size(ALL), 128))
    notes = lax.all_to_all(sent, ALL, 0, 0, tiled=True).reshape(dp_count, 2, 4, 128)
    raw = merged(notes[..., :share], 1) - jnp.sum(notes[..., share : 2 * share], axis=1)
    seqs = seq_lengths.shape[0]
    lengths = notes[:, 0, 0, 2 * share : 2 * share + seqs]
    labels = notes[:, 0, 0, 2 * share + seqs : 2 * share + 2 * seqs]
    raw = raw.reshape(dp_count, seqs, SEQ_LEN)
    valid = jnp.arange(SEQ_LEN, dtype=jnp.float32) < lengths[..., None]
    token_loss = jnp.where(valid, raw, 0.0)
    seq_loss = jnp.sum(token_loss, axis=2)
    hot = (labels[..., None] == jnp.arange(DOMAINS, dtype=jnp.float32)).astype(jnp.float32)
    domain_loss = jnp.sum(hot * seq_loss[..., None], axis=(0, 1))
    domain_count = jnp.sum(hot * lengths[..., None], axis=(0, 1))
    probability = (1.0 - DOMAINS * explore_share) * domain_weights / jnp.sum(
        domain_weights
    ) + explore_share
    reward = domain_loss / jnp.maximum(domain_count, 1.0) / probability
    raised = domain_weights * jnp.exp(step_rate * reward)
    new_weights = DOMAINS * raised / jnp.sum(raised)
    mine_loss = lax.dynamic_index_in_dim(token_loss, dp_index, 0, keepdims=False).reshape(-1)
    return (mine_loss, new_weights)


def solution(mesh):
    torus = Mesh(mesh.devices.reshape(8, 4, 2, 2, 2), ALL)
    in_specs = (P(DP, None), P(None, ALL), P(), P(DP), P(DP), P())
    out_specs = (P(DP), P())
    return jax.shard_map(body, mesh=torus, in_specs=in_specs, out_specs=out_specs, check_vma=False)
```

```python
import functools
import jax
import jax.numpy as jnp
from jax import lax
from jax.experimental import pallas as pl
from jax.experimental.pallas import tpu as pltpu
from jax.sharding import Mesh
from jax.sharding import PartitionSpec as P

SEQ_LEN = 16
DOMAINS = 22
explore_share = 0.01
step_rate = 0.002

ALL = ("z", "x", "yh", "yl", "c")
DP = ("z", "x")
VOCAB_AXES = ("yh", "yl", "c")
SUB = 16
VMEM_LIMIT = 60 * 2**20


def shift(a, axis, by):
    n = lax.axis_size(axis)
    return lax.ppermute(a, axis, [(i, (i + by) % n) for i in range(n)])


def together(*arrays):
    return lax.optimization_barrier(arrays)


def onward(a, axis):
    n = lax.axis_size(axis)
    moves = [
        (i * 2 + core, ((i + (1 if core == 0 else -1)) % n) * 2 + core)
        for i in range(n)
        for core in range(2)
    ]
    return lax.ppermute(a, (axis, "c"), moves)


def mirrored(a, axis):
    return jnp.roll(jnp.flip(a, axis), 1, axis)


def lane_parts(a):
    return [a[:, i : i + 128] for i in range(0, a.shape[1], 128)]


def stats_kernel(pieces, chunks, has_prev, others, starts, targets, *refs):
    n_arrays = 1 + max(p[0] for p in pieces)
    refs = list(refs)
    arrays = [refs.pop(0) for _ in range(n_arrays)]
    cols = [[refs.pop(0) for _ in range(n)] for n in chunks]
    prev = refs.pop(0) if has_prev else None
    earlier = [refs.pop(0) for _ in others]
    out, h_vm, w_vm, t_vm, m_vm, s_vm, p_vm, h_sem, w_sem = refs
    width = cols[0][0].shape[1]
    total = sum(p[2] for p in pieces)
    padded = m_vm.shape[0]
    h_copies, at = [], 0
    for i, (k, first, n, _) in enumerate(pieces):
        h_copies.append(
            pltpu.make_async_copy(
                arrays[k].at[pl.ds(first, n)], h_vm.at[pl.ds(at, n)], h_sem.at[i]
            )
        )
        at += n
    w_copies, used = [], 0
    for k, chunk_refs in enumerate(cols):
        copies, depth = [], 0
        for w in chunk_refs:
            to = w_vm.at[pl.ds(depth, w.shape[0]), pl.ds(k * width, width)]
            copies.append(pltpu.make_async_copy(w, to, w_sem.at[used]))
            depth += w.shape[0]
            used += 1
        w_copies.append(copies)
    for copy in h_copies + sum(w_copies, []):
        copy.start()
    spread = jnp.broadcast_to(targets[...].astype(jnp.float32), (128, padded))
    t_vm[...] = spread.T.astype(jnp.int32)
    if padded > total:
        rest = pl.ds(total, padded - total)
        for ref in (m_vm, s_vm, p_vm):
            ref[rest] = jnp.zeros((padded - total, 128), jnp.float32)
    for copy in h_copies:
        copy.wait()
    here = pl.ds(0, total)
    for k in range(len(cols)):
        for copy in w_copies[k]:
            copy.wait()
        logits = jnp.dot(
            h_vm[...], w_vm[:, k * width : (k + 1) * width], preferred_element_type=jnp.float32
        )
        parts = lane_parts(logits)
        peak = functools.reduce(jnp.maximum, parts)
        if k:
            before = m_vm[here]
            peak = jnp.maximum(peak, before)
            mass = s_vm[here] * jnp.exp(before - peak)
            pick = p_vm[here]
        else:
            mass = jnp.zeros_like(peak)
            pick = jnp.zeros_like(peak)
        away = t_vm[here] - lax.broadcasted_iota(jnp.int32, peak.shape, 1)
        for i, part in enumerate(parts):
            column = starts[k] + i * 128
            mass = mass + jnp.exp(part - peak)
            pick = pick + jnp.where(away == column, part, 0.0)
        m_vm[here] = peak
        s_vm[here] = mass
        p_vm[here] = pick

    lane_peak = m_vm[...].T
    peak = jnp.max(lane_peak, axis=0, keepdims=True)
    mass = jnp.sum(s_vm[...].T * jnp.exp(lane_peak - peak), axis=0, keepdims=True)
    pick = jnp.sum(p_vm[...].T, axis=0, keepdims=True)
    if has_prev:
        joined = jnp.maximum(peak, prev[0:1, :])
        mass = mass * jnp.exp(peak - joined) + jnp.exp(prev[0:1, :] - joined)
        pick = pick + prev[1:2, :]
        peak = joined
    lse = peak + jnp.log(mass)
    if not others:
        out[0:1, :] = lse
        out[1:2, :] = pick
        return
    z, x, sign = (starts[len(cols) + i] for i in range(3))
    out[:, : 4 * SUB] = jnp.full((out.shape[0], 4 * SUB), -1e30, jnp.float32)
    out[:, 4 * SUB :] = jnp.zeros((out.shape[0], 4 * SUB), jnp.float32)
    found = [([s for p in pieces for s in p[3]], lse, pick)]
    found += [(subs, ref[0:1, :], ref[1:2, :]) for subs, ref in zip(others, earlier)]
    for subs, all_lse, all_pick in found:
        for i, (mz, mx, part, half) in enumerate(subs):
            row = lax.rem(z + mz * sign + 8, 8) * 4 + lax.rem(x + mx * sign + 4, 4)
            lanes = slice(i * SUB, (i + 1) * SUB)
            to = (part * 2 + half) * SUB
            out[pl.ds(row, 1), to : to + SUB] = all_lse[:, lanes]
            out[pl.ds(row, 1), 4 * SUB + to : 5 * SUB + to] = all_pick[:, lanes]


def wanted_of(targets, subs):
    picked = jnp.concatenate([targets[mz % 8, mx % 4, part, half] for mz, mx, part, half in subs])
    return jnp.pad(picked, (0, -picked.shape[0] % 128)).reshape(1, -1)


def tile_stats(pieces, wanted, cols, scalars, prev=None, others=()):
    arrays, listed = [], []
    for array, first, n, subs in pieces:
        for k, known in enumerate(arrays):
            if known is array:
                break
        else:
            k = len(arrays)
            arrays.append(array)
        listed.append((k, first, n, tuple(subs)))
    flat = sum(cols, [])
    depth, width = sum(w.shape[0] for w in cols[0]), flat[0].shape[1]
    n_cols = len(cols) * width
    total = sum(p[2] for p in listed)
    padded = -(-total // 128) * 128
    in_vmem = pl.BlockSpec(memory_space=pltpu.VMEM)
    any_spec = pl.BlockSpec(memory_space=pl.ANY)
    operands = [scalars, wanted, *arrays, *flat]
    in_specs = [pl.BlockSpec(memory_space=pltpu.SMEM), in_vmem]
    in_specs += [any_spec] * (len(arrays) + len(flat))
    if prev is not None:
        operands.append(prev)
        in_specs.append(in_vmem)
    for _, stats in others:
        operands.append(stats)
        in_specs.append(in_vmem)
    shape = (32, 8 * SUB) if others else (2, padded)
    subs = [s for p in listed for s in p[3]]
    stats = pl.pallas_call(
        functools.partial(
            stats_kernel, tuple(listed), tuple(len(w) for w in cols), prev is not None, tuple(o[0] for o in others)
        ),
        out_shape=jax.ShapeDtypeStruct(shape, jnp.float32),
        in_specs=in_specs,
        out_specs=in_vmem,
        scratch_shapes=[
            pltpu.VMEM((total, depth), jnp.bfloat16),
            pltpu.VMEM((depth, n_cols), jnp.bfloat16),
            pltpu.VMEM((padded, 128), jnp.int32),
            pltpu.VMEM((padded, 128), jnp.float32),
            pltpu.VMEM((padded, 128), jnp.float32),
            pltpu.VMEM((padded, 128), jnp.float32),
            pltpu.SemaphoreType.DMA((len(listed),)),
            pltpu.SemaphoreType.DMA((len(flat),)),
        ],
        compiler_params=pltpu.CompilerParams(vmem_limit_bytes=VMEM_LIMIT),
        cost_estimate=pl.CostEstimate(
            flops=2 * total * depth * n_cols,
            bytes_accessed=2 * depth * (total + n_cols),
            transcendentals=total * n_cols,
        ),
    )(*operands)
    return tuple(subs), stats


def finish_kernel(place, notes, weights, loss_out, weights_out, loss_vm, sum_vm, count_vm):
    n = notes[...]
    twin = pltpu.roll(n, 4, 1)
    top = jnp.maximum(n, twin)
    lse = top + jnp.log(jnp.exp(n - top) + jnp.exp(twin - top))
    raw = lse - pltpu.roll(n + twin, 96, 2)
    core_row = lax.broadcasted_iota(jnp.int32, (1, 8, 128), 1)
    lane = lax.broadcasted_iota(jnp.int32, (1, 8, 128), 2)
    seq = (core_row // 2) * 4 + (lane // SEQ_LEN) * 2 + core_row % 2
    position = lane % SEQ_LEN
    live = jnp.logical_and(core_row < 4, lane < 2 * SEQ_LEN)
    length = jnp.zeros_like(n)
    label = jnp.full(n.shape, -1.0, jnp.float32)
    for k in range(8):
        here = jnp.logical_and(seq == k, live)
        length = jnp.where(here, n[:, 0:1, 64 + k : 65 + k], length)
        label = jnp.where(here, n[:, 0:1, 72 + k : 73 + k], label)
    loss = jnp.where(position.astype(jnp.float32) < length, raw, 0.0)
    count = jnp.where(position == 0, length, 0.0)
    loss_vm[...] = loss
    sum_vm[...] = jnp.zeros_like(sum_vm)
    count_vm[...] = jnp.zeros_like(count_vm)
    for d in range(DOMAINS):
        inside = label == float(d)
        sum_d = jnp.sum(jnp.where(inside, loss, 0.0), axis=0)
        count_d = jnp.sum(jnp.where(inside, count, 0.0), axis=0)
        sum_vm[d : d + 1, :] = jnp.sum(sum_d, axis=0, keepdims=True)
        count_vm[d : d + 1, :] = jnp.sum(count_d, axis=0, keepdims=True)
    domain_loss = jnp.sum(sum_vm[...], axis=1, keepdims=True)
    domain_count = jnp.sum(count_vm[...], axis=1, keepdims=True)
    w = weights[...]
    probability = (1.0 - DOMAINS * explore_share) * w / jnp.sum(w, axis=0, keepdims=True)
    probability = probability + explore_share
    reward = domain_loss / jnp.maximum(domain_count, 1.0) / probability
    raised = w * jnp.exp(step_rate * reward)
    weights_out[...] = DOMAINS * raised / jnp.sum(raised, axis=0, keepdims=True)
    mine = loss_vm[place[0]]
    for row in range(4):
        for part in range(2):
            to = ((row // 2) * 4 + part * 2 + row % 2) * SEQ_LEN
            loss_out[:, to : to + SEQ_LEN] = mine[
                row : row + 1, part * SEQ_LEN : (part + 1) * SEQ_LEN
            ]


def rolled(a, axis, by):
    n = a.shape[axis]
    twice = jnp.concatenate([a, a], axis=axis)
    return lax.dynamic_slice_in_dim(twice, by, n, axis)


def merged(lse, axis):
    top = jnp.max(lse, axis=axis, keepdims=True)
    return jnp.squeeze(top, axis) + jnp.log(jnp.sum(jnp.exp(lse - top), axis=axis))


def body(hidden_states, head_weight, target_ids, seq_lengths, domain_labels, domain_weights):
    z, x = lax.axis_index("z"), lax.axis_index("x")
    yh, yl, c = (lax.axis_index(a) for a in VOCAB_AXES)
    nz, nx = lax.axis_size("z"), lax.axis_size("x")
    dp_count = nz * nx
    dp_index = z * nx + x
    y = yh * 2 + yl
    width = head_weight.shape[1]
    sign = 1 - 2 * c

    targets = target_ids.reshape(nz, nx, 2, 2, 2, SUB)
    targets = lax.dynamic_index_in_dim(targets, yl, 2, keepdims=False)
    targets = rolled(rolled(targets, 0, z), 1, x)
    other = jnp.flip(mirrored(mirrored(targets, 0), 1), 3)
    targets = jnp.where(c == 0, targets, other)

    def start_of(y_at, core):
        return (dp_index * 8 + (y_at % 4) * 2 + core) * width

    def start_in(core):
        return jnp.where(core == 0, start_of(y + 3, 0), start_of(y + 1, 1))

    own_starts = [start_of(y, c), start_of(y, 1 - c)]
    in_starts = [start_in(c), start_in(1 - c)]

    def scalars(*values):
        return jnp.stack(values).astype(jnp.int32)

    def rows_of(part, half):
        first = (yl * 4 + part * 2 + half) * SUB
        return lax.dynamic_slice_in_dim(hidden_states, first, SUB, 0)

    moves = [
        (k * 2 + core, ((k + (1 if core == 0 else -1)) % 4) * 2 + core)
        for k in range(4)
        for core in range(2)
    ]
    def moved(subs, dz, dx):
        return [(mz + dz, mx + dx, part, half) for mz, mx, part, half in subs]

    def mates(subs):
        return [(-mz, -mx, part, 1 - half) for mz, mx, part, half in subs]

    subs_a = [(0, 0, 0, 0), (0, -1, 0, 0), (0, -1, 0, 1), (0, -2, 0, 0)]
    subs_b1 = [(0, 0, 1, 0), (-1, 0, 1, 0), (-1, 0, 1, 1), (-2, 0, 1, 0), (-2, 0, 1, 1)]
    subs_b2 = [(-3, 0, 1, 0), (-3, 0, 1, 1), (-4, 0, 1, 0)]

    mine_1 = [
        subs_a,
        subs_b1,
        moved(subs_a, -1, 0),
        moved(mates(subs_a), -1, 0),
        moved(subs_b1, 0, -1),
        moved(mates(subs_b1), 0, -1),
        subs_b2[:2],
    ]
    mine_3 = [
        moved(subs_a, -2, 0),
        moved(mates(subs_a), -2, 0),
        moved(subs_b1, 0, -2),
        subs_b2[2:],
    ]
    mine_4 = [
        moved(subs_a, -3, 0),
        moved(mates(subs_a), -3, 0),
        moved(subs_b2, 0, -1),
        moved(mates(subs_b2), 0, -1),
        moved(subs_a, -4, 0),
        moved(subs_b2, 0, -2),
    ]
    subs_1, subs_3, subs_4 = (sum(m, []) for m in (mine_1, mine_3, mine_4))

    def pieces_of(arrays, subs):
        return [(a, 0, a.shape[0], s) for a, s in zip(arrays, subs)]

    col_in = lax.ppermute(head_weight, VOCAB_AXES, moves)
    own_a = jnp.concatenate([rows_of(0, c), rows_of(0, 1 - c)], axis=0)
    own_b = jnp.concatenate([rows_of(1, c), rows_of(1, 1 - c)], axis=0)
    xa1, zb1 = onward(own_a, "x"), onward(own_b, "z")
    xa1, zb1 = together(xa1, zb1)
    xa2, zb2 = onward(xa1[:SUB], "x"), onward(zb1, "z")
    xa2, zb2, late_w = together(xa2, zb2, head_weight)
    mine_a = jnp.concatenate([own_a[:SUB], xa1, xa2], axis=0)
    mine_b1 = jnp.concatenate([own_b[:SUB], zb1, zb2], axis=0)
    xb1, za1 = onward(mine_b1, "x"), onward(mine_a, "z")
    mate_b1, mate_a = shift(mine_b1, "c", 1), shift(mine_a, "c", 1)
    wanted = [wanted_of(targets, subs) for subs in (subs_1, subs_3, subs_4)]
    xb1_mate, za1_mate, zb3 = onward(mate_b1, "x"), onward(mate_a, "z"), onward(zb2, "z")
    col_mate = shift(late_w, "c", 1)
    xb1, za1, xb1_mate, za1_mate, zb3, col_mate, col_in, *wanted = together(
        xb1, za1, xb1_mate, za1_mate, zb3, col_mate, col_in, *wanted
    )
    za2, za2_mate = onward(za1, "z"), onward(za1_mate, "z")
    xb2, zb4 = onward(xb1, "x"), onward(zb3[:SUB], "z")

    pieces = pieces_of([mine_a, mine_b1, za1, za1_mate, xb1, xb1_mate, zb3], mine_1)
    near_cols = [[head_weight], [col_mate]]
    _, stats_1 = tile_stats(pieces, wanted[0], near_cols, scalars(*own_starts))
    za2, za2_mate, xb2, zb4, stats_1 = together(za2, za2_mate, xb2, zb4, stats_1)
    za3, za3_mate = onward(za2, "z"), onward(za2_mate, "z")
    mine_b2 = jnp.concatenate([zb3, zb4], axis=0)
    mate_b2 = shift(mine_b2, "c", 1)
    xb3, xb3_mate = onward(mine_b2, "x"), onward(mate_b2, "x")
    col_in_mate = shift(col_in, "c", 1)
    far_cols = [[col_in], [col_in_mate]]
    done_1 = tile_stats(pieces, wanted[0], far_cols, scalars(*in_starts), prev=stats_1)
    stats_2 = done_1[1]
    za3, za3_mate, xb3, xb3_mate, stats_2 = together(za3, za3_mate, xb3, xb3_mate, stats_2)
    za4, xb4 = onward(za3, "z"), onward(xb3, "x")
    cols = near_cols + far_cols
    pieces = pieces_of([za2, za2_mate, xb2, zb4], mine_3)
    done_2 = tile_stats(pieces, wanted[1], cols, scalars(*own_starts, *in_starts))
    stats_3 = done_2[1]
    za4, xb4, stats_3 = together(za4, xb4, stats_3)
    pieces = pieces_of([za3, za3_mate, xb3, xb3_mate, za4, xb4], mine_4)
    _, every = tile_stats(
        pieces,
        wanted[2],
        cols,
        scalars(*own_starts, *in_starts, z, x, sign),
        others=[(done_1[0], stats_2), (done_2[0], stats_3)],
    )
    share = 4 * SUB
    mine = lax.all_to_all(every, DP, 0, 0, tiled=True)
    found = jnp.concatenate([merged(mine[:, :share], 0), jnp.sum(mine[:, share:], axis=0)])
    halves = found.reshape(2, 2, 2, SUB)
    rest = jnp.flip(shift(found, "c", 1).reshape(2, 2, 2, SUB), 2)
    lse = merged(jnp.stack([halves[0, :, 0], rest[0, :, 0]]), 0).reshape(-1)
    pick = (halves[1, :, 0] + rest[1, :, 0]).reshape(-1)
    note = jnp.concatenate(
        [lse, pick, seq_lengths.astype(jnp.float32), domain_labels.astype(jnp.float32)]
    )
    note = jnp.pad(note, (0, 128 - note.shape[0]))
    sent = jnp.broadcast_to(note[None], (lax.axis_size(ALL), 128))
    notes = lax.all_to_all(sent, ALL, 0, 0, tiled=True)
    weights = jnp.pad(domain_weights, (0, 32 - DOMAINS)).reshape(32, 1)
    token_loss, new_weights = pl.pallas_call(
        finish_kernel,
        out_shape=(
            jax.ShapeDtypeStruct((1, 128), jnp.float32),
            jax.ShapeDtypeStruct((32, 1), jnp.float32),
        ),
        in_specs=[
            pl.BlockSpec(memory_space=pltpu.SMEM),
            pl.BlockSpec(memory_space=pltpu.VMEM),
            pl.BlockSpec(memory_space=pltpu.VMEM),
        ],
        out_specs=(
            pl.BlockSpec(memory_space=pltpu.VMEM),
            pl.BlockSpec(memory_space=pltpu.VMEM),
        ),
        scratch_shapes=[
            pltpu.VMEM((dp_count, 8, 128), jnp.float32),
            pltpu.VMEM((32, 128), jnp.float32),
            pltpu.VMEM((32, 128), jnp.float32),
        ],
    )(dp_index.reshape(1), notes.reshape(dp_count, 8, 128), weights)
    return (token_loss.reshape(-1), new_weights[:DOMAINS, 0])


def solution(mesh):
    torus = Mesh(mesh.devices.reshape(8, 4, 2, 2, 2), ALL)
    in_specs = (P(DP, None), P(None, ALL), P(), P(DP), P(DP), P())
    out_specs = (P(DP), P())
    return jax.shard_map(body, mesh=torus, in_specs=in_specs, out_specs=out_specs, check_vma=False)
```

```python
import functools
import jax
import jax.numpy as jnp
from jax import lax
from jax.experimental import pallas as pl
from jax.experimental.pallas import tpu as pltpu
from jax.sharding import Mesh
from jax.sharding import PartitionSpec as P

SEQ_LEN = 16
DOMAINS = 22
explore_share = 0.01
step_rate = 0.002

ALL = ("z", "x", "yh", "yl", "c")
DP = ("z", "x")
VOCAB_AXES = ("yh", "yl", "c")
SUB = 16


def shift(a, axis, by):
    n = lax.axis_size(axis)
    return lax.ppermute(a, axis, [(i, (i + by) % n) for i in range(n)])


def together(*arrays):
    return lax.optimization_barrier(arrays)


def onward(a, axis):
    n = lax.axis_size(axis)
    moves = [
        (i * 2 + core, ((i + (1 if core == 0 else -1)) % n) * 2 + core)
        for i in range(n)
        for core in range(2)
    ]
    return lax.ppermute(a, (axis, "c"), moves)


def mirrored(a, axis):
    return jnp.roll(jnp.flip(a, axis), 1, axis)


def lane_parts(a):
    return [a[:, i : i + 128] for i in range(0, a.shape[1], 128)]


def stats_kernel(pieces, chunks, has_prev, others, starts, targets, *refs):
    n_arrays = 1 + max(p[0] for p in pieces)
    refs = list(refs)
    arrays = [refs.pop(0) for _ in range(n_arrays)]
    cols = [[refs.pop(0) for _ in range(n)] for n in chunks]
    prev = refs.pop(0) if has_prev else None
    earlier = [refs.pop(0) for _ in others]
    out, h_vm, w_vm, t_vm, m_vm, s_vm, p_vm, h_sem, w_sem = refs
    width = cols[0][0].shape[1]
    total = sum(p[2] for p in pieces)
    padded = m_vm.shape[0]
    h_copies, at = [], 0
    for i, (k, first, n, _) in enumerate(pieces):
        h_copies.append(
            pltpu.make_async_copy(
                arrays[k].at[pl.ds(first, n)], h_vm.at[pl.ds(at, n)], h_sem.at[i]
            )
        )
        at += n
    w_copies, used = [], 0
    for k, chunk_refs in enumerate(cols):
        copies, depth = [], 0
        for w in chunk_refs:
            to = w_vm.at[pl.ds(depth, w.shape[0]), pl.ds(k * width, width)]
            copies.append(pltpu.make_async_copy(w, to, w_sem.at[used]))
            depth += w.shape[0]
            used += 1
        w_copies.append(copies)
    for copy in h_copies + sum(w_copies, []):
        copy.start()
    spread = jnp.broadcast_to(targets[...].astype(jnp.float32), (128, padded))
    t_vm[...] = spread.T.astype(jnp.int32)
    if padded > total:
        rest = pl.ds(total, padded - total)
        for ref in (m_vm, s_vm, p_vm):
            ref[rest] = jnp.zeros((padded - total, 128), jnp.float32)
    for copy in h_copies:
        copy.wait()
    here = pl.ds(0, total)
    for k in range(len(cols)):
        for copy in w_copies[k]:
            copy.wait()
        logits = jnp.dot(
            h_vm[...], w_vm[:, k * width : (k + 1) * width], preferred_element_type=jnp.float32
        )
        parts = lane_parts(logits)
        peak = functools.reduce(jnp.maximum, parts)
        if k:
            before = m_vm[here]
            peak = jnp.maximum(peak, before)
            mass = s_vm[here] * jnp.exp(before - peak)
            pick = p_vm[here]
        else:
            mass = jnp.zeros_like(peak)
            pick = jnp.zeros_like(peak)
        away = t_vm[here] - lax.broadcasted_iota(jnp.int32, peak.shape, 1)
        for i, part in enumerate(parts):
            column = starts[k] + i * 128
            mass = mass + jnp.exp(part - peak)
            pick = pick + jnp.where(away == column, part, 0.0)
        m_vm[here] = peak
        s_vm[here] = mass
        p_vm[here] = pick

    lane_peak = m_vm[...].T
    peak = jnp.max(lane_peak, axis=0, keepdims=True)
    mass = jnp.sum(s_vm[...].T * jnp.exp(lane_peak - peak), axis=0, keepdims=True)
    pick = jnp.sum(p_vm[...].T, axis=0, keepdims=True)
    if has_prev:
        joined = jnp.maximum(peak, prev[0:1, :])
        mass = mass * jnp.exp(peak - joined) + jnp.exp(prev[0:1, :] - joined)
        pick = pick + prev[1:2, :]
        peak = joined
    lse = peak + jnp.log(mass)
    if not others:
        out[0:1, :] = lse
        out[1:2, :] = pick
        return
    z, x, sign = (starts[len(cols) + i] for i in range(3))
    out[:, : 4 * SUB] = jnp.full((out.shape[0], 4 * SUB), -1e30, jnp.float32)
    out[:, 4 * SUB :] = jnp.zeros((out.shape[0], 4 * SUB), jnp.float32)
    found = [([s for p in pieces for s in p[3]], lse, pick)]
    found += [(subs, ref[0:1, :], ref[1:2, :]) for subs, ref in zip(others, earlier)]
    for subs, all_lse, all_pick in found:
        for i, (mz, mx, part, half) in enumerate(subs):
            row = lax.rem(z + mz * sign + 8, 8) * 4 + lax.rem(x + mx * sign + 4, 4)
            lanes = slice(i * SUB, (i + 1) * SUB)
            to = (part * 2 + half) * SUB
            out[pl.ds(row, 1), to : to + SUB] = all_lse[:, lanes]
            out[pl.ds(row, 1), 4 * SUB + to : 5 * SUB + to] = all_pick[:, lanes]


def wanted_of(targets, subs):
    picked = jnp.concatenate([targets[mz % 8, mx % 4, part, half] for mz, mx, part, half in subs])
    return jnp.pad(picked, (0, -picked.shape[0] % 128)).reshape(1, -1)


def tile_stats(pieces, wanted, cols, scalars, prev=None, others=()):
    arrays, listed = [], []
    for array, first, n, subs in pieces:
        for k, known in enumerate(arrays):
            if known is array:
                break
        else:
            k = len(arrays)
            arrays.append(array)
        listed.append((k, first, n, tuple(subs)))
    flat = sum(cols, [])
    depth, width = sum(w.shape[0] for w in cols[0]), flat[0].shape[1]
    n_cols = len(cols) * width
    total = sum(p[2] for p in listed)
    padded = -(-total // 128) * 128
    in_vmem = pl.BlockSpec(memory_space=pltpu.VMEM)
    any_spec = pl.BlockSpec(memory_space=pl.ANY)
    operands = [scalars, wanted, *arrays, *flat]
    in_specs = [pl.BlockSpec(memory_space=pltpu.SMEM), in_vmem]
    in_specs += [any_spec] * (len(arrays) + len(flat))
    if prev is not None:
        operands.append(prev)
        in_specs.append(in_vmem)
    for _, stats in others:
        operands.append(stats)
        in_specs.append(in_vmem)
    shape = (32, 8 * SUB) if others else (2, padded)
    subs = [s for p in listed for s in p[3]]
    stats = pl.pallas_call(
        functools.partial(
            stats_kernel, tuple(listed), tuple(len(w) for w in cols), prev is not None, tuple(o[0] for o in others)
        ),
        out_shape=jax.ShapeDtypeStruct(shape, jnp.float32),
        in_specs=in_specs,
        out_specs=in_vmem,
        scratch_shapes=[
            pltpu.VMEM((total, depth), jnp.bfloat16),
            pltpu.VMEM((depth, n_cols), jnp.bfloat16),
            pltpu.VMEM((padded, 128), jnp.int32),
            pltpu.VMEM((padded, 128), jnp.float32),
            pltpu.VMEM((padded, 128), jnp.float32),
            pltpu.VMEM((padded, 128), jnp.float32),
            pltpu.SemaphoreType.DMA((len(listed),)),
            pltpu.SemaphoreType.DMA((len(flat),)),
        ],
        compiler_params=pltpu.CompilerParams(vmem_limit_bytes=60 * 2**20),
        cost_estimate=pl.CostEstimate(
            flops=2 * total * depth * n_cols,
            bytes_accessed=2 * depth * (total + n_cols),
            transcendentals=total * n_cols,
        ),
    )(*operands)
    return tuple(subs), stats


def finish_kernel(place, notes, weights, loss_out, weights_out, loss_vm, sum_vm, count_vm):
    n = notes[...]
    twin = pltpu.roll(n, 4, 1)
    top = jnp.maximum(n, twin)
    lse = top + jnp.log(jnp.exp(n - top) + jnp.exp(twin - top))
    raw = lse - pltpu.roll(n + twin, 96, 2)
    core_row = lax.broadcasted_iota(jnp.int32, (1, 8, 128), 1)
    lane = lax.broadcasted_iota(jnp.int32, (1, 8, 128), 2)
    seq = (core_row // 2) * 4 + (lane // SEQ_LEN) * 2 + core_row % 2
    position = lane % SEQ_LEN
    live = jnp.logical_and(core_row < 4, lane < 2 * SEQ_LEN)
    length = jnp.zeros_like(n)
    label = jnp.full(n.shape, -1.0, jnp.float32)
    for k in range(8):
        here = jnp.logical_and(seq == k, live)
        length = jnp.where(here, n[:, 0:1, 64 + k : 65 + k], length)
        label = jnp.where(here, n[:, 0:1, 72 + k : 73 + k], label)
    loss = jnp.where(position.astype(jnp.float32) < length, raw, 0.0)
    count = jnp.where(position == 0, length, 0.0)
    loss_vm[...] = loss
    sum_vm[...] = jnp.zeros_like(sum_vm)
    count_vm[...] = jnp.zeros_like(count_vm)
    for d in range(DOMAINS):
        inside = label == float(d)
        sum_d = jnp.sum(jnp.where(inside, loss, 0.0), axis=0)
        count_d = jnp.sum(jnp.where(inside, count, 0.0), axis=0)
        sum_vm[d : d + 1, :] = jnp.sum(sum_d, axis=0, keepdims=True)
        count_vm[d : d + 1, :] = jnp.sum(count_d, axis=0, keepdims=True)
    domain_loss = jnp.sum(sum_vm[...].T, axis=0, keepdims=True)
    domain_count = jnp.sum(count_vm[...].T, axis=0, keepdims=True)
    w = weights[...]
    probability = (1.0 - DOMAINS * explore_share) * w / jnp.sum(w, axis=1, keepdims=True)
    probability = probability + explore_share
    reward = domain_loss / jnp.maximum(domain_count, 1.0) / probability
    raised = w * jnp.exp(step_rate * reward)
    scaled = DOMAINS * raised / jnp.sum(raised, axis=1, keepdims=True)
    weights_out[...] = scaled[:, :DOMAINS]
    mine = loss_vm[place[0]]
    for row in range(4):
        for part in range(2):
            to = ((row // 2) * 4 + part * 2 + row % 2) * SEQ_LEN
            loss_out[:, to : to + SEQ_LEN] = mine[
                row : row + 1, part * SEQ_LEN : (part + 1) * SEQ_LEN
            ]


def rolled(a, axis, by):
    n = a.shape[axis]
    twice = jnp.concatenate([a, a], axis=axis)
    return lax.dynamic_slice_in_dim(twice, by, n, axis)


def merged(lse, axis):
    top = jnp.max(lse, axis=axis, keepdims=True)
    return jnp.squeeze(top, axis) + jnp.log(jnp.sum(jnp.exp(lse - top), axis=axis))


def body(hidden_states, head_weight, target_ids, seq_lengths, domain_labels, domain_weights):
    z, x = lax.axis_index("z"), lax.axis_index("x")
    yh, yl, c = (lax.axis_index(a) for a in VOCAB_AXES)
    nz, nx = lax.axis_size("z"), lax.axis_size("x")
    dp_count = nz * nx
    dp_index = z * nx + x
    y = yh * 2 + yl
    width = head_weight.shape[1]
    sign = 1 - 2 * c

    targets = target_ids.reshape(nz, nx, 2, 2, 2, SUB)
    targets = lax.dynamic_index_in_dim(targets, yl, 2, keepdims=False)
    targets = rolled(rolled(targets, 0, z), 1, x)
    other = jnp.flip(mirrored(mirrored(targets, 0), 1), 3)
    targets = jnp.where(c == 0, targets, other)

    def start_of(y_at, core):
        return (dp_index * 8 + (y_at % 4) * 2 + core) * width

    def start_in(core):
        return jnp.where(core == 0, start_of(y + 3, 0), start_of(y + 1, 1))

    own_starts = [start_of(y, c), start_of(y, 1 - c)]
    in_starts = [start_in(c), start_in(1 - c)]

    def scalars(*values):
        return jnp.stack(values).astype(jnp.int32)

    def rows_of(part, half):
        first = (yl * 4 + part * 2 + half) * SUB
        return lax.dynamic_slice_in_dim(hidden_states, first, SUB, 0)

    moves = [
        (k * 2 + core, ((k + (1 if core == 0 else -1)) % 4) * 2 + core)
        for k in range(4)
        for core in range(2)
    ]
    def moved(subs, dz, dx):
        return [(mz + dz, mx + dx, part, half) for mz, mx, part, half in subs]

    def mates(subs):
        return [(-mz, -mx, part, 1 - half) for mz, mx, part, half in subs]

    subs_a = [(0, 0, 0, 0), (0, -1, 0, 0), (0, -1, 0, 1), (0, -2, 0, 0)]
    subs_b1 = [(0, 0, 1, 0), (-1, 0, 1, 0), (-1, 0, 1, 1), (-2, 0, 1, 0), (-2, 0, 1, 1)]
    subs_b2 = [(-3, 0, 1, 0), (-3, 0, 1, 1), (-4, 0, 1, 0)]

    mine_1 = [
        subs_a,
        subs_b1,
        moved(subs_a, -1, 0) + subs_b2[:2],
        moved(mates(subs_a), -1, 0),
        moved(subs_b1, 0, -1),
        moved(mates(subs_b1), 0, -1),
    ]
    mine_4 = [
        moved(subs_a, -2, 0) + subs_b2[2:],
        moved(mates(subs_a), -2, 0),
        moved(subs_b1, 0, -2),
        moved(subs_a, -3, 0),
        moved(mates(subs_a), -3, 0),
        moved(subs_b2, 0, -1),
        moved(mates(subs_b2), 0, -1),
        moved(subs_a, -4, 0),
        moved(subs_b2, 0, -2),
    ]
    subs_1, subs_4 = sum(mine_1, []), sum(mine_4, [])

    def pieces_of(arrays, subs):
        return [(a, 0, len(s) * SUB, s) for a, s in zip(arrays, subs)]

    col_in = lax.ppermute(head_weight, VOCAB_AXES, moves)
    own_a = jnp.concatenate([rows_of(0, c), rows_of(0, 1 - c)], axis=0)
    own_b = jnp.concatenate([rows_of(1, c), rows_of(1, 1 - c)], axis=0)
    xa1, zb1 = onward(own_a, "x"), onward(own_b, "z")
    col_mate = shift(head_weight, "c", 1)
    xa1, zb1, col_mate = together(xa1, zb1, col_mate)
    xa2, zb2 = onward(xa1[:SUB], "x"), onward(zb1, "z")
    xa2, zb2 = together(xa2, zb2)
    mine_a = jnp.concatenate([own_a[:SUB], xa1, xa2], axis=0)
    mine_b1 = jnp.concatenate([own_b[:SUB], zb1, zb2], axis=0)
    riding = jnp.concatenate([own_a[:SUB], xa1, xa2, zb2], axis=0)
    xb1, za1 = onward(mine_b1, "x"), onward(riding, "z")
    mate_b1, mate_a = shift(mine_b1, "c", 1), shift(mine_a, "c", 1)
    wanted = [wanted_of(targets, subs) for subs in (subs_1, subs_4)]
    xb1_mate, za1_mate = onward(mate_b1, "x"), onward(mate_a, "z")
    xb1, za1, xb1_mate, za1_mate, col_in, *wanted = together(
        xb1, za1, xb1_mate, za1_mate, col_in, *wanted
    )
    za2, za2_mate = onward(za1, "z"), onward(za1_mate, "z")
    xb2 = onward(xb1, "x")

    pieces = pieces_of([mine_a, mine_b1, za1, za1_mate, xb1, xb1_mate], mine_1)
    near_cols = [[head_weight], [col_mate]]
    _, stats_1 = tile_stats(pieces, wanted[0], near_cols, scalars(*own_starts))
    za2, za2_mate, xb2, stats_1 = together(za2, za2_mate, xb2, stats_1)
    za3, za3_mate = onward(za2[: 4 * SUB], "z"), onward(za2_mate, "z")
    mine_b2 = jnp.concatenate([za1[4 * SUB :], za2[4 * SUB : 5 * SUB]], axis=0)
    mate_b2 = shift(mine_b2, "c", 1)
    xb3, xb3_mate = onward(mine_b2, "x"), onward(mate_b2, "x")
    col_in_mate = shift(col_in, "c", 1)
    far_cols = [[col_in], [col_in_mate]]
    done_1 = tile_stats(pieces, wanted[0], far_cols, scalars(*in_starts), prev=stats_1)
    stats_2 = done_1[1]
    za3, xb3, stats_2 = together(za3, xb3, stats_2)
    za4, xb4 = onward(za3, "z"), onward(xb3, "x")
    cols = near_cols + far_cols
    pieces = pieces_of(
        [za2, za2_mate, xb2, za3, za3_mate, xb3, xb3_mate, za4, xb4], mine_4
    )
    _, every = tile_stats(
        pieces,
        wanted[1],
        cols,
        scalars(*own_starts, *in_starts, z, x, sign),
        others=[(done_1[0], stats_2)],
    )
    share = 4 * SUB
    mine = lax.all_to_all(every, DP, 0, 0, tiled=True)
    found = jnp.concatenate([merged(mine[:, :share], 0), jnp.sum(mine[:, share:], axis=0)])
    halves = found.reshape(2, 2, 2, SUB)
    rest = jnp.flip(shift(found, "c", 1).reshape(2, 2, 2, SUB), 2)
    lse = merged(jnp.stack([halves[0, :, 0], rest[0, :, 0]]), 0).reshape(-1)
    pick = (halves[1, :, 0] + rest[1, :, 0]).reshape(-1)
    note = jnp.concatenate(
        [lse, pick, seq_lengths.astype(jnp.float32), domain_labels.astype(jnp.float32)]
    )
    note = jnp.pad(note, (0, 128 - note.shape[0]))
    sent = jnp.broadcast_to(note[None], (lax.axis_size(ALL), 128))
    notes = lax.all_to_all(sent, ALL, 0, 0, tiled=True)
    weights = jnp.pad(domain_weights, (0, 128 - DOMAINS)).reshape(1, 128)
    token_loss, new_weights = pl.pallas_call(
        finish_kernel,
        out_shape=(
            jax.ShapeDtypeStruct((1, 128), jnp.float32),
            jax.ShapeDtypeStruct((1, DOMAINS), jnp.float32),
        ),
        in_specs=[
            pl.BlockSpec(memory_space=pltpu.SMEM),
            pl.BlockSpec(memory_space=pltpu.VMEM),
            pl.BlockSpec(memory_space=pltpu.VMEM),
        ],
        out_specs=(
            pl.BlockSpec(memory_space=pltpu.VMEM),
            pl.BlockSpec(memory_space=pltpu.VMEM),
        ),
        scratch_shapes=[
            pltpu.VMEM((dp_count, 8, 128), jnp.float32),
            pltpu.VMEM((128, 128), jnp.float32),
            pltpu.VMEM((128, 128), jnp.float32),
        ],
    )(dp_index.reshape(1), notes.reshape(dp_count, 8, 128), weights)
    return (token_loss.reshape(-1), new_weights.reshape(-1))


def solution(mesh):
    torus = Mesh(mesh.devices.reshape(8, 4, 2, 2, 2), ALL)
    in_specs = (P(DP, None), P(None, ALL), P(), P(DP), P(DP), P())
    out_specs = (P(DP), P())
    return jax.shard_map(body, mesh=torus, in_specs=in_specs, out_specs=out_specs, check_vma=False)
```

```python
import functools
import jax
import jax.numpy as jnp
from jax import lax
from jax.experimental import pallas as pl
from jax.experimental.pallas import tpu as pltpu
from jax.sharding import Mesh
from jax.sharding import PartitionSpec as P

SEQ_LEN = 16
DOMAINS = 22
explore_share = 0.01
step_rate = 0.002

ALL = ("z", "x", "yh", "yl", "c")
DP = ("z", "x")
VOCAB_AXES = ("yh", "yl", "c")
SUB = 16


def shift(a, axis, by):
    n = lax.axis_size(axis)
    return lax.ppermute(a, axis, [(i, (i + by) % n) for i in range(n)])


def together(*arrays):
    return lax.optimization_barrier(arrays)


def onward(a, axis):
    n = lax.axis_size(axis)
    moves = [
        (i * 2 + core, ((i + (1 if core == 0 else -1)) % n) * 2 + core)
        for i in range(n)
        for core in range(2)
    ]
    return lax.ppermute(a, (axis, "c"), moves)


def mirrored(a, axis):
    return jnp.roll(jnp.flip(a, axis), 1, axis)


def lane_parts(a):
    return [a[:, i : i + 128] for i in range(0, a.shape[1], 128)]


def stats_kernel(pieces, chunks, has_prev, others, starts, targets, *refs):
    n_arrays = 1 + max(p[0] for p in pieces)
    refs = list(refs)
    arrays = [refs.pop(0) for _ in range(n_arrays)]
    cols = [[refs.pop(0) for _ in range(n)] for n in chunks]
    prev = refs.pop(0) if has_prev else None
    earlier = [refs.pop(0) for _ in others]
    out, h_vm, w_vm, t_vm, m_vm, s_vm, p_vm, h_sem, w_sem = refs
    width = cols[0][0].shape[1]
    total = sum(p[2] for p in pieces)
    padded = m_vm.shape[0]
    h_copies, at = [], 0
    for i, (k, first, n, _) in enumerate(pieces):
        h_copies.append(
            pltpu.make_async_copy(
                arrays[k].at[pl.ds(first, n)], h_vm.at[pl.ds(at, n)], h_sem.at[i]
            )
        )
        at += n
    w_copies, used = [], 0
    for k, chunk_refs in enumerate(cols):
        copies, depth = [], 0
        for w in chunk_refs:
            to = w_vm.at[pl.ds(depth, w.shape[0]), pl.ds(k * width, width)]
            copies.append(pltpu.make_async_copy(w, to, w_sem.at[used]))
            depth += w.shape[0]
            used += 1
        w_copies.append(copies)
    for copy in h_copies + sum(w_copies, []):
        copy.start()
    spread = jnp.broadcast_to(targets[...].astype(jnp.float32), (128, padded))
    t_vm[...] = spread.T.astype(jnp.int32)
    if padded > total:
        rest = pl.ds(total, padded - total)
        for ref in (m_vm, s_vm, p_vm):
            ref[rest] = jnp.zeros((padded - total, 128), jnp.float32)
    for copy in h_copies:
        copy.wait()
    here = pl.ds(0, total)
    for k in range(len(cols)):
        for copy in w_copies[k]:
            copy.wait()
        logits = jnp.dot(
            h_vm[...], w_vm[:, k * width : (k + 1) * width], preferred_element_type=jnp.float32
        )
        parts = lane_parts(logits)
        peak = functools.reduce(jnp.maximum, parts)
        if k:
            before = m_vm[here]
            peak = jnp.maximum(peak, before)
            mass = s_vm[here] * jnp.exp(before - peak)
            pick = p_vm[here]
        else:
            mass = jnp.zeros_like(peak)
            pick = jnp.zeros_like(peak)
        away = t_vm[here] - lax.broadcasted_iota(jnp.int32, peak.shape, 1)
        for i, part in enumerate(parts):
            column = starts[k] + i * 128
            mass = mass + jnp.exp(part - peak)
            pick = pick + jnp.where(away == column, part, 0.0)
        m_vm[here] = peak
        s_vm[here] = mass
        p_vm[here] = pick

    lane_peak = m_vm[...].T
    peak = jnp.max(lane_peak, axis=0, keepdims=True)
    mass = jnp.sum(s_vm[...].T * jnp.exp(lane_peak - peak), axis=0, keepdims=True)
    pick = jnp.sum(p_vm[...].T, axis=0, keepdims=True)
    if has_prev:
        joined = jnp.maximum(peak, prev[0:1, :])
        mass = mass * jnp.exp(peak - joined) + jnp.exp(prev[0:1, :] - joined)
        pick = pick + prev[1:2, :]
        peak = joined
    lse = peak + jnp.log(mass)
    if not others:
        out[0:1, :] = lse
        out[1:2, :] = pick
        return
    z, x, sign = (starts[len(cols) + i] for i in range(3))
    out[:, : 4 * SUB] = jnp.full((out.shape[0], 4 * SUB), -1e30, jnp.float32)
    out[:, 4 * SUB :] = jnp.zeros((out.shape[0], 4 * SUB), jnp.float32)
    found = [([s for p in pieces for s in p[3]], lse, pick)]
    found += [(subs, ref[0:1, :], ref[1:2, :]) for subs, ref in zip(others, earlier)]
    for subs, all_lse, all_pick in found:
        for i, (mz, mx, part, half) in enumerate(subs):
            row = lax.rem(z + mz * sign + 8, 8) * 4 + lax.rem(x + mx * sign + 4, 4)
            lanes = slice(i * SUB, (i + 1) * SUB)
            to = (part * 2 + half) * SUB
            out[pl.ds(row, 1), to : to + SUB] = all_lse[:, lanes]
            out[pl.ds(row, 1), 4 * SUB + to : 5 * SUB + to] = all_pick[:, lanes]


def wanted_of(targets, subs):
    picked = jnp.concatenate([targets[mz % 8, mx % 4, part, half] for mz, mx, part, half in subs])
    return jnp.pad(picked, (0, -picked.shape[0] % 128)).reshape(1, -1)


def tile_stats(pieces, wanted, cols, scalars, prev=None, others=()):
    arrays, listed = [], []
    for array, first, n, subs in pieces:
        for k, known in enumerate(arrays):
            if known is array:
                break
        else:
            k = len(arrays)
            arrays.append(array)
        listed.append((k, first, n, tuple(subs)))
    flat = sum(cols, [])
    depth, width = sum(w.shape[0] for w in cols[0]), flat[0].shape[1]
    n_cols = len(cols) * width
    total = sum(p[2] for p in listed)
    padded = -(-total // 128) * 128
    in_vmem = pl.BlockSpec(memory_space=pltpu.VMEM)
    any_spec = pl.BlockSpec(memory_space=pl.ANY)
    operands = [scalars, wanted, *arrays, *flat]
    in_specs = [pl.BlockSpec(memory_space=pltpu.SMEM), in_vmem]
    in_specs += [any_spec] * (len(arrays) + len(flat))
    if prev is not None:
        operands.append(prev)
        in_specs.append(in_vmem)
    for _, stats in others:
        operands.append(stats)
        in_specs.append(in_vmem)
    shape = (32, 8 * SUB) if others else (2, padded)
    subs = [s for p in listed for s in p[3]]
    stats = pl.pallas_call(
        functools.partial(
            stats_kernel, tuple(listed), tuple(len(w) for w in cols), prev is not None, tuple(o[0] for o in others)
        ),
        out_shape=jax.ShapeDtypeStruct(shape, jnp.float32),
        in_specs=in_specs,
        out_specs=in_vmem,
        scratch_shapes=[
            pltpu.VMEM((total, depth), jnp.bfloat16),
            pltpu.VMEM((depth, n_cols), jnp.bfloat16),
            pltpu.VMEM((padded, 128), jnp.int32),
            pltpu.VMEM((padded, 128), jnp.float32),
            pltpu.VMEM((padded, 128), jnp.float32),
            pltpu.VMEM((padded, 128), jnp.float32),
            pltpu.SemaphoreType.DMA((len(listed),)),
            pltpu.SemaphoreType.DMA((len(flat),)),
        ],
        compiler_params=pltpu.CompilerParams(vmem_limit_bytes=60 * 2**20),
        cost_estimate=pl.CostEstimate(
            flops=2 * total * depth * n_cols,
            bytes_accessed=2 * depth * (total + n_cols),
            transcendentals=total * n_cols,
        ),
    )(*operands)
    return tuple(subs), stats


def finish_kernel(place, notes, weights, loss_out, weights_out, loss_vm, sum_vm, count_vm):
    n = notes[...]
    twin = pltpu.roll(n, 4, 1)
    top = jnp.maximum(n, twin)
    lse = top + jnp.log(jnp.exp(n - top) + jnp.exp(twin - top))
    raw = lse - pltpu.roll(n + twin, 96, 2)
    core_row = lax.broadcasted_iota(jnp.int32, (1, 8, 128), 1)
    lane = lax.broadcasted_iota(jnp.int32, (1, 8, 128), 2)
    seq = (core_row // 2) * 4 + (lane // SEQ_LEN) * 2 + core_row % 2
    position = lane % SEQ_LEN
    live = jnp.logical_and(core_row < 4, lane < 2 * SEQ_LEN)
    length = jnp.zeros_like(n)
    label = jnp.full(n.shape, -1.0, jnp.float32)
    for k in range(8):
        here = jnp.logical_and(seq == k, live)
        length = jnp.where(here, n[:, 0:1, 64 + k : 65 + k], length)
        label = jnp.where(here, n[:, 0:1, 72 + k : 73 + k], label)
    loss = jnp.where(position.astype(jnp.float32) < length, raw, 0.0)
    count = jnp.where(position == 0, length, 0.0)
    loss_vm[...] = loss
    sum_vm[...] = jnp.zeros_like(sum_vm)
    count_vm[...] = jnp.zeros_like(count_vm)
    for d in range(DOMAINS):
        inside = label == float(d)
        sum_d = jnp.sum(jnp.where(inside, loss, 0.0), axis=0)
        count_d = jnp.sum(jnp.where(inside, count, 0.0), axis=0)
        sum_vm[d : d + 1, :] = jnp.sum(sum_d, axis=0, keepdims=True)
        count_vm[d : d + 1, :] = jnp.sum(count_d, axis=0, keepdims=True)
    domain_loss = jnp.sum(sum_vm[...].T, axis=0, keepdims=True)
    domain_count = jnp.sum(count_vm[...].T, axis=0, keepdims=True)
    w = weights[...]
    probability = (1.0 - DOMAINS * explore_share) * w / jnp.sum(w, axis=1, keepdims=True)
    probability = probability + explore_share
    reward = domain_loss / jnp.maximum(domain_count, 1.0) / probability
    raised = w * jnp.exp(step_rate * reward)
    scaled = DOMAINS * raised / jnp.sum(raised, axis=1, keepdims=True)
    weights_out[...] = scaled[:, :DOMAINS]
    mine = loss_vm[place[0]]
    for row in range(4):
        for part in range(2):
            to = ((row // 2) * 4 + part * 2 + row % 2) * SEQ_LEN
            loss_out[:, to : to + SEQ_LEN] = mine[
                row : row + 1, part * SEQ_LEN : (part + 1) * SEQ_LEN
            ]


def rolled(a, axis, by):
    n = a.shape[axis]
    twice = jnp.concatenate([a, a], axis=axis)
    return lax.dynamic_slice_in_dim(twice, by, n, axis)


def merged(lse, axis):
    top = jnp.max(lse, axis=axis, keepdims=True)
    return jnp.squeeze(top, axis) + jnp.log(jnp.sum(jnp.exp(lse - top), axis=axis))


def body(hidden_states, head_weight, target_ids, seq_lengths, domain_labels, domain_weights):
    z, x = lax.axis_index("z"), lax.axis_index("x")
    yh, yl, c = (lax.axis_index(a) for a in VOCAB_AXES)
    nz, nx = lax.axis_size("z"), lax.axis_size("x")
    dp_count = nz * nx
    dp_index = z * nx + x
    y = yh * 2 + yl
    width = head_weight.shape[1]
    sign = 1 - 2 * c

    targets = target_ids.reshape(nz, nx, 2, 2, 2, SUB)
    targets = lax.dynamic_index_in_dim(targets, yl, 2, keepdims=False)
    targets = rolled(rolled(targets, 0, z), 1, x)
    other = jnp.flip(mirrored(mirrored(targets, 0), 1), 3)
    targets = jnp.where(c == 0, targets, other)

    def start_of(y_at, core):
        return (dp_index * 8 + (y_at % 4) * 2 + core) * width

    def start_in(core):
        return jnp.where(core == 0, start_of(y + 3, 0), start_of(y + 1, 1))

    own_starts = [start_of(y, c), start_of(y, 1 - c)]
    in_starts = [start_in(c), start_in(1 - c)]

    def scalars(*values):
        return jnp.stack(values).astype(jnp.int32)

    def rows_of(part, half):
        first = (yl * 4 + part * 2 + half) * SUB
        return lax.dynamic_slice_in_dim(hidden_states, first, SUB, 0)

    moves = [
        (k * 2 + core, ((k + (1 if core == 0 else -1)) % 4) * 2 + core)
        for k in range(4)
        for core in range(2)
    ]
    def moved(subs, dz, dx):
        return [(mz + dz, mx + dx, part, half) for mz, mx, part, half in subs]

    def mates(subs):
        return [(-mz, -mx, part, 1 - half) for mz, mx, part, half in subs]

    subs_a = [(0, 0, 0, 0), (0, -1, 0, 0), (0, -1, 0, 1), (0, -2, 0, 0)]
    subs_b1 = [(0, 0, 1, 0), (-1, 0, 1, 0), (-1, 0, 1, 1), (-2, 0, 1, 0), (-2, 0, 1, 1)]
    subs_b2 = [(-3, 0, 1, 0), (-3, 0, 1, 1), (-4, 0, 1, 0)]

    mine_1 = [
        subs_a,
        subs_b1,
        moved(subs_a, -1, 0) + subs_b2[:2],
        moved(mates(subs_a), -1, 0),
        moved(subs_b1, 0, -1),
        moved(mates(subs_b1), 0, -1),
    ]
    mine_4 = [
        moved(subs_a, -2, 0) + subs_b2[2:],
        moved(mates(subs_a), -2, 0),
        moved(subs_b1, 0, -2),
        moved(subs_a, -3, 0),
        moved(mates(subs_a), -3, 0),
        moved(subs_b2, 0, -1),
        moved(mates(subs_b2), 0, -1),
        moved(subs_a, -4, 0),
        moved(subs_b2, 0, -2),
    ]
    subs_1, subs_4 = sum(mine_1, []), sum(mine_4, [])

    def pieces_of(arrays, subs):
        return [(a, 0, len(s) * SUB, s) for a, s in zip(arrays, subs)]

    col_in = lax.ppermute(head_weight, VOCAB_AXES, moves)
    own_a = jnp.concatenate([rows_of(0, c), rows_of(0, 1 - c)], axis=0)
    own_b = jnp.concatenate([rows_of(1, c), rows_of(1, 1 - c)], axis=0)
    xa1, zb1 = onward(own_a, "x"), onward(own_b, "z")
    col_mate = shift(head_weight, "c", 1)
    xa1, zb1, col_mate = together(xa1, zb1, col_mate)
    xa2, zb2 = onward(xa1[:SUB], "x"), onward(zb1, "z")
    xa2, zb2 = together(xa2, zb2)
    mine_a = jnp.concatenate([own_a[:SUB], xa1, xa2], axis=0)
    mine_b1 = jnp.concatenate([own_b[:SUB], zb1, zb2], axis=0)
    riding = jnp.concatenate([own_a[:SUB], xa1, xa2, zb2], axis=0)
    xb1, za1 = onward(mine_b1, "x"), onward(riding, "z")
    mate_b1, mate_a = shift(mine_b1, "c", 1), shift(mine_a, "c", 1)
    wanted = [wanted_of(targets, subs) for subs in (subs_1, subs_4)]
    xb1_mate, za1_mate = onward(mate_b1, "x"), onward(mate_a, "z")
    xb1, za1, xb1_mate, za1_mate, col_in, *wanted = together(
        xb1, za1, xb1_mate, za1_mate, col_in, *wanted
    )
    za2, za2_mate = onward(za1, "z"), onward(za1_mate, "z")
    xb2 = onward(xb1, "x")

    pieces = pieces_of([mine_a, mine_b1, za1, za1_mate, xb1, xb1_mate], mine_1)
    near_cols = [[head_weight], [col_mate]]
    _, stats_1 = tile_stats(pieces, wanted[0], near_cols, scalars(*own_starts))
    za2, za2_mate, xb2, stats_1 = together(za2, za2_mate, xb2, stats_1)
    za3, za3_mate = onward(za2[: 4 * SUB], "z"), onward(za2_mate, "z")
    mine_b2 = jnp.concatenate([za1[4 * SUB :], za2[4 * SUB : 5 * SUB]], axis=0)
    mate_b2 = shift(mine_b2, "c", 1)
    xb3, xb3_mate = onward(mine_b2, "x"), onward(mate_b2, "x")
    col_in_mate = shift(col_in, "c", 1)
    far_cols = [[col_in], [col_in_mate]]
    za3, xb3, far_starts = together(za3, xb3, scalars(*in_starts))
    za4, xb4 = onward(za3, "z"), onward(xb3, "x")
    done_1 = tile_stats(pieces, wanted[0], far_cols, far_starts, prev=stats_1)
    stats_2 = done_1[1]
    cols = near_cols + far_cols
    pieces = pieces_of(
        [za2, za2_mate, xb2, za3, za3_mate, xb3, xb3_mate, za4, xb4], mine_4
    )
    _, every = tile_stats(
        pieces,
        wanted[1],
        cols,
        scalars(*own_starts, *in_starts, z, x, sign),
        others=[(done_1[0], stats_2)],
    )
    share = 4 * SUB
    mine = lax.all_to_all(every, DP, 0, 0, tiled=True)
    found = jnp.concatenate([merged(mine[:, :share], 0), jnp.sum(mine[:, share:], axis=0)])
    halves = found.reshape(2, 2, 2, SUB)
    rest = jnp.flip(shift(found, "c", 1).reshape(2, 2, 2, SUB), 2)
    lse = merged(jnp.stack([halves[0, :, 0], rest[0, :, 0]]), 0).reshape(-1)
    pick = (halves[1, :, 0] + rest[1, :, 0]).reshape(-1)
    note = jnp.concatenate(
        [lse, pick, seq_lengths.astype(jnp.float32), domain_labels.astype(jnp.float32)]
    )
    note = jnp.pad(note, (0, 128 - note.shape[0]))
    sent = jnp.broadcast_to(note[None], (lax.axis_size(ALL), 128))
    notes = lax.all_to_all(sent, ALL, 0, 0, tiled=True)
    weights = jnp.pad(domain_weights, (0, 128 - DOMAINS)).reshape(1, 128)
    token_loss, new_weights = pl.pallas_call(
        finish_kernel,
        out_shape=(
            jax.ShapeDtypeStruct((1, 128), jnp.float32),
            jax.ShapeDtypeStruct((1, DOMAINS), jnp.float32),
        ),
        in_specs=[
            pl.BlockSpec(memory_space=pltpu.SMEM),
            pl.BlockSpec(memory_space=pltpu.VMEM),
            pl.BlockSpec(memory_space=pltpu.VMEM),
        ],
        out_specs=(
            pl.BlockSpec(memory_space=pltpu.VMEM),
            pl.BlockSpec(memory_space=pltpu.VMEM),
        ),
        scratch_shapes=[
            pltpu.VMEM((dp_count, 8, 128), jnp.float32),
            pltpu.VMEM((128, 128), jnp.float32),
            pltpu.VMEM((128, 128), jnp.float32),
        ],
    )(dp_index.reshape(1), notes.reshape(dp_count, 8, 128), weights)
    return (token_loss.reshape(-1), new_weights.reshape(-1))


def solution(mesh):
    torus = Mesh(mesh.devices.reshape(8, 4, 2, 2, 2), ALL)
    in_specs = (P(DP, None), P(None, ALL), P(), P(DP), P(DP), P())
    out_specs = (P(DP), P())
    return jax.shard_map(body, mesh=torus, in_specs=in_specs, out_specs=out_specs, check_vma=False)
```
